1024 devices in a mesh: dp: 64 (over x, y, core), own: 16 (over z).
Axes of the slice: x: 4, y: 8, z: 16, core: 2. Of those that a mesh axis runs over, the one named last changes fastest.
Arguments:
- embeddings: bfloat16 [131072, 4096], P(('dp', 'own')), may hold values from -16 to 16
- coarse_ids: int32 [131072], P(('dp', 'own')), may hold values from 0 to 255, as said below
- fine_cents: bfloat16 [16384, 4096], P('dp'), may hold values from -3 to 3
- coarse_prev: bfloat16 [256, 4096], P('dp'), may hold values from -3 to 3
Outputs:
- fine_next: float32 [16384, 4096], P('dp', 'own')
- weight_totals: float32 [16384], P('dp')
- coarse_next: bfloat16 [256, 4096], replicated
The draws below stay inside these ranges and needn't reach their ends.
Inputs may be any that keep to these rules, and one draw needn't show every extreme that they name: `coarse_ids`: cluster c belongs to owner group c // 4. Within the 128 rows of one device, at most 4 rows name clusters of any one owner group, and some owner group is named by exactly 4 of them.
All inputs are finite; a program needn't handle non-finite values.
Results may differ from the reference program's by a relative error of at most 0.013.
Values may be sent and summed in bfloat16 or wider, within the bound.
A program may use at most 32 MiB of HBM per device.

```python
import math
import jax
import jax.numpy as jnp
from jax import lax

D = 4096
FINE_PER = 64
CLU_DEV = 4
ROWS_DEV = 128
TOKENS = 131072
COARSE = 256
FINES = 16384
CAP = 4
N_DP = 64
N_OWN = 16


def route_ids(key):
    key = jax.random.fold_in(key, 7)
    slots = 2 * ROWS_DEV
    blocks = TOKENS // ROWS_DEV

    def one_block(block_key):
        key_hot, key_perm, key_rows, key_local = jax.random.split(block_key, 4)
        hot = jax.random.randint(key_hot, (), 0, N_DP)
        scores = jax.random.permutation(key_perm, slots).astype(jnp.int32)
        owner_of = jnp.arange(slots, dtype=jnp.int32) // CAP
        scores = scores + jnp.where(owner_of == hot, -slots, 0)
        chosen = jnp.argsort(scores, stable=True)[:ROWS_DEV].astype(jnp.int32)
        owners = jax.random.permutation(key_rows, chosen // CAP)
        return owners * CLU_DEV + jax.random.randint(key_local, (ROWS_DEV,), 0, CLU_DEV)
    return jax.vmap(one_block)(jax.random.split(key, blocks)).reshape(-1).astype(jnp.int32)


def fine_table(key, spread):
    values = jax.random.normal(jax.random.fold_in(key, 11), (FINES, D), jnp.float32) * 0.5
    factor = 1.0 + spread * (jax.random.uniform(jax.random.fold_in(key, 12), (FINES, 1), jnp.float32) - 0.5)
    return jnp.clip(values * factor, -3.0, 3.0)


def coarse_table(key, spread):
    values = jax.random.normal(jax.random.fold_in(key, 13), (COARSE, D), jnp.float32) * 0.5
    factor = 1.0 + spread * (jax.random.uniform(jax.random.fold_in(key, 14), (COARSE, 1), jnp.float32) - 0.5)
    return jnp.clip(values * factor, -3.0, 3.0)


def draw_coarse_ids(key, part):
    return route_ids(key)


def draw_fine_cents(key, part):
    table = fine_table(key, 0.0)
    return table.astype(jnp.bfloat16)


def draw_coarse_prev(key, part):
    table = coarse_table(key, 0.0)
    return table.astype(jnp.bfloat16)


def draw_embeddings(key, part):
    key = jax.random.fold_in(key, 5)
    key_drawn = jax.random.fold_in(key, 4)
    values = jax.random.normal(key_drawn, (TOKENS, D), jnp.float32)
    return jnp.clip(values, -16.0, 16.0).astype(jnp.bfloat16)


def setup_inputs(seed: int = 0) -> dict:
    key_of = jax.random.split(jax.random.key(seed), 5)
    embeddings = draw_embeddings(jax.random.fold_in(key_of[4], 71), 0)
    coarse_ids = draw_coarse_ids(jax.random.fold_in(key_of[4], 71), 0)
    fine_cents = draw_fine_cents(jax.random.fold_in(key_of[4], 71), 0)
    coarse_prev = draw_coarse_prev(jax.random.fold_in(key_of[4], 71), 0)
    return dict(embeddings=embeddings, coarse_ids=coarse_ids, fine_cents=fine_cents, coarse_prev=coarse_prev)


def soft_stats(rows_in, local, valid, fines, fsq, coarse, scale):
    pick = (local[:, None] == jnp.arange(coarse.shape[0], dtype=jnp.int32)[None, :]).astype(jnp.bfloat16)
    base = jnp.dot(pick, coarse, preferred_element_type=jnp.float32)
    resid = (rows_in.astype(jnp.float32) - base).astype(jnp.bfloat16)
    prod = lax.dot_general(resid, fines, (((1,), (1,)), ((), ())), preferred_element_type=jnp.float32)
    logits = (prod - 0.5 * fsq[None, :]) * scale
    owned = (jnp.arange(fines.shape[0], dtype=jnp.int32) // FINE_PER)[None, :] == local[:, None]
    logits = jnp.where(owned, logits, jnp.float32(-1e+30))
    top = lax.optimization_barrier(jnp.max(logits, axis=1, keepdims=True))
    expo = jnp.exp(logits - top)
    probs = expo / lax.optimization_barrier(jnp.sum(expo, axis=1, keepdims=True)) * valid[:, None].astype(jnp.float32)
    weights = probs.astype(jnp.bfloat16)
    stats = lax.dot_general(weights, resid, (((0,), (0,)), ((), ())), preferred_element_type=jnp.float32)
    return (stats, lax.optimization_barrier(jnp.sum(probs, axis=0)))

def reference(embeddings, coarse_ids, fine_cents, coarse_prev):
    rows = embeddings.shape[0]
    width = embeddings.shape[1]
    group_fines = CLU_DEV * FINE_PER
    segment = 2 * ROWS_DEV
    scale = 4.0 / math.sqrt(width)
    group = coarse_ids // CLU_DEV
    member = jnp.arange(rows, dtype=jnp.int32) // ROWS_DEV % N_OWN
    label = (group * N_OWN + member).astype(jnp.int32)
    order = jnp.argsort(label, stable=True).astype(jnp.int32)
    counts = jax.ops.segment_sum(jnp.ones((rows,), jnp.int32), label, num_segments=N_DP * N_OWN)
    starts = (jnp.cumsum(counts) - counts).astype(jnp.int32)
    sorted_rows = jnp.concatenate([embeddings[order], jnp.zeros((segment, width), jnp.bfloat16)], axis=0)
    sorted_ids = jnp.concatenate([coarse_ids[order], jnp.zeros((segment,), jnp.int32)], axis=0)

    def one_group(index):
        fines = lax.dynamic_slice_in_dim(fine_cents, (index * group_fines).astype(jnp.int32), group_fines, 0)
        coarse = lax.dynamic_slice_in_dim(coarse_prev, (index * CLU_DEV).astype(jnp.int32), CLU_DEV, 0)
        fsq = lax.optimization_barrier(jnp.sum(jnp.square(fines.astype(jnp.float32)), axis=1))

        def one_member(carry, slot):
            spot = index * N_OWN + slot
            start = starts[spot]
            count = counts[spot]
            block = lax.dynamic_slice_in_dim(sorted_rows, start.astype(jnp.int32), segment, 0)
            tags = lax.dynamic_slice_in_dim(sorted_ids, start.astype(jnp.int32), segment, 0)
            valid = jnp.arange(segment, dtype=jnp.int32) < count
            local = jnp.where(valid, tags - index * CLU_DEV, 0).astype(jnp.int32)
            stats, mass = soft_stats(block, local, valid, fines, fsq, coarse, scale)
            rounded = lax.optimization_barrier(stats.astype(jnp.bfloat16)).astype(jnp.float32)
            return ((carry[0] + rounded, carry[1] + mass), None)
        init = (jnp.zeros((group_fines, width), jnp.float32), jnp.zeros((group_fines,), jnp.float32))
        (sums, mass), _ = lax.scan(one_member, init, jnp.arange(N_OWN, dtype=jnp.int32))
        fresh = (4.0 * fines.astype(jnp.float32) + sums) / (4.0 + mass[:, None])
        coarse_new = (coarse.astype(jnp.float32) + lax.optimization_barrier(jnp.mean(fresh.reshape(CLU_DEV, FINE_PER, width), axis=1))).astype(jnp.bfloat16)
        return (fresh, mass, coarse_new)
    fresh, mass, coarse_new = lax.map(one_group, jnp.arange(N_DP, dtype=jnp.int32))
    return (fresh.reshape(-1, width), mass.reshape(-1), coarse_new.reshape(-1, width))
```

```python
import functools
import math

import jax
import jax.numpy as jnp
from jax import lax
from jax.experimental import pallas as pl
from jax.experimental.pallas import tpu as pltpu
from jax.sharding import PartitionSpec as P

MESH = pl.DeviceIdType.MESH
FINE_PER = 64
CLU_DEV = 4
CAP = 4
PARTS = 4
BLK = CAP * PARTS
N_X = 4
SUBS = 2
F32 = jnp.float32
BF16 = jnp.bfloat16


def drain(ref, sem):
    pltpu.make_async_copy(ref, ref, sem).wait()


def iota(shape, dim):
    return lax.broadcasted_iota(jnp.int32, shape, dim)


def kernel(
    n_x,
    n_y,
    n_z,
    emb_hbm,
    ids_ref,
    fines_hbm,
    coarse_ref,
    fine_out,
    tot_out,
    coarse_out,
    emb,
    fines,
    outbox,
    inbox,
    ids_box,
    ids_f,
    resid,
    stats,
    rs_src,
    rs_buf,
    tot_box,
    cpart,
    cbox,
    zbox,
    own_piece,
    block,
    agbuf,
    load_sem,
    ids_send,
    ids_recv,
    a2a_send,
    a2a_recv,
    rs_send,
    rs_recv,
    st_send,
    st_recv,
):
    n_dp = 2 * n_x * n_y
    rows, width = emb_hbm.shape
    part = width // PARTS
    group_fines = fines.shape[0]
    cols = width // n_z
    n_h = cols // 128
    scale = 4.0 / math.sqrt(width)

    me = lax.axis_index("dp")
    z = lax.axis_index("own")
    core = lax.rem(me, 2)
    chip = lax.div(me, 2)
    y = lax.rem(chip, n_y)
    x = lax.div(chip, n_y)

    def send(src, dst, send_sem, recv_sem, **to):
        copy = pltpu.make_async_remote_copy(
            src_ref=src,
            dst_ref=dst,
            send_sem=send_sem,
            recv_sem=recv_sem,
            device_id=to,
            device_id_type=MESH,
        )
        copy.start()

    def z_peers(body):
        @pl.loop(1, n_z)
        def _(k):
            body(lax.rem(z + k, n_z))

    barrier = pltpu.get_barrier_semaphore()

    loads = []
    for p in range(PARTS):
        loads.append(
            pltpu.make_async_copy(
                emb_hbm.at[:, pl.ds(p * part, part)],
                emb.at[pl.ds(p * rows, rows)],
                load_sem.at[p],
            )
        )
    loads.append(pltpu.make_async_copy(fines_hbm, fines, load_sem.at[PARTS]))
    for load in loads:
        load.start()

    @pl.loop(1, n_dp)
    def _(k):
        pl.semaphore_signal(
            barrier, inc=1, device_id={"dp": lax.rem(me + k, n_dp)}, device_id_type=MESH
        )

    @pl.loop(1, n_z)
    def _(k):
        pl.semaphore_signal(
            barrier, inc=1, device_id={"own": lax.rem(z + k, n_z)}, device_id_type=MESH
        )

    ids = ids_ref[0]
    owner = ids >> 2
    owner_rows = jnp.broadcast_to(owner.astype(F32), (rows, rows))
    eye = iota((rows, rows), 0) == iota((rows, rows), 1)
    before = iota((rows, rows), 0) < iota((rows, rows), 1)
    owner_col = jnp.sum(jnp.where(eye, owner_rows, 0.0), axis=1, keepdims=True)
    same = jnp.where(before & (owner_col == owner_rows), 1.0, 0.0)
    rank = jnp.sum(same, axis=0, keepdims=True).astype(jnp.int32)
    y_bits = n_y.bit_length() - 1
    to_core = owner & 1
    to_y = (owner >> 1) & (n_y - 1)
    to_x = owner >> (1 + y_bits)
    dxi = (to_x - x + 2 * n_x - 1) & (n_x - 1)
    dy = (to_y - y + n_y) & (n_y - 1)
    half = n_y // 2
    dyi = jnp.where(dy >= half, 2 * (dy - half), 2 * (half - dy) - 1)
    place = ((to_core * n_x + dxi) * n_y + dyi) * BLK + rank
    target = jnp.concatenate([place + p * CAP for p in range(PARTS)], axis=1)

    ids_box[n_dp - 2] = ids
    for load in loads[:PARTS]:
        load.wait()
    pl.semaphore_wait(barrier, n_dp - 1 + n_z - 1)

    chunk = n_y * BLK

    @pl.loop(0, 2 * n_x)
    def _(jc):
        base = pl.multiple_of(jc * chunk, chunk)
        hot = (iota((chunk, PARTS * rows), 0) + base == target).astype(F32).astype(BF16)
        outbox[pl.ds(base, chunk), :] = jnp.dot(
            hot, emb[...], preferred_element_type=F32
        ).astype(BF16)
        dest_core = lax.div(jc, n_x)
        at_x = lax.rem(jc, n_x)
        dest_x = lax.rem(x + at_x + 1, n_x)
        flip = lax.rem(dest_core + core, 2)
        for at_y in range(n_y):
            step = (at_y + 1) // 2
            delta = (n_y // 2 + (step if at_y % 2 == 0 else -step)) % n_y
            dest = (dest_x * n_y + lax.rem(y + delta, n_y)) * 2 + dest_core
            slot = (at_x * n_y + at_y) * 2 + flip
            src = outbox.at[pl.ds(pl.multiple_of(base + at_y * BLK, BLK), BLK)]
            dst = inbox.at[pl.ds(pl.multiple_of(slot * BLK, BLK), BLK)]

            def post():
                send(ids_ref.at[0], ids_box.at[slot], ids_send, ids_recv, dp=dest)
                send(src, dst, a2a_send, a2a_recv.at[at_x], dp=dest)

            if at_y < n_y - 1:
                post()
            else:
                mine = (at_x == n_x - 1) & (flip == 0)
                pl.when(jnp.logical_not(mine))(post)

                @pl.when(mine)
                def _():
                    pltpu.make_async_copy(src, dst, a2a_recv.at[at_x]).start()

    loads[PARTS].wait()
    fsq_col = jnp.sum(jnp.square(fines[...].astype(F32)), axis=1, keepdims=True)
    eye_f = iota((group_fines, group_fines), 0) == iota((group_fines, group_fines), 1)
    fsq = jnp.sum(jnp.where(eye_f, fsq_col, 0.0), axis=0, keepdims=True)

    drain(ids_box.at[pl.ds(0, n_dp - 1)], ids_recv)
    for i in range(n_dp):
        ids_f[pl.ds(i, 1), :] = ids_box[i].astype(F32)
    slots = n_dp * CAP
    spread = (iota((slots, n_dp), 0) >> 2) == iota((slots, n_dp), 1)
    seen = jnp.dot(
        spread.astype(F32).astype(BF16), ids_f[...].astype(BF16), preferred_element_type=F32
    )
    low = (me * CLU_DEV).astype(F32)
    ours = jnp.where((seen >= low) & (seen < low + CLU_DEV), 1.0, 0.0)
    order = jnp.dot(
        ours.astype(BF16), before.astype(F32).astype(BF16), preferred_element_type=F32
    )
    nth = (iota((slots, rows), 0) & (CAP - 1)).astype(F32)
    tag = jnp.sum(
        jnp.where(order == nth, ours * (seen - low + 1.0), 0.0), axis=1, keepdims=True
    )

    src_b = 2 * n_y
    rows_b = src_b * CAP
    out_row = iota((src_b * BLK, src_b * BLK), 0)
    in_row = iota((src_b * BLK, src_b * BLK), 1)
    quarter = lax.div(out_row, rows_b)
    within = lax.rem(out_row, rows_b)
    perm = (in_row == (within >> 2) * BLK + quarter * CAP + (within & 3)).astype(F32).astype(BF16)
    for b in range(n_x):
        arrived = inbox.at[pl.ds(b * src_b * BLK, src_b * BLK)]
        drain(arrived, a2a_recv.at[b])
        flat = jnp.dot(perm, arrived[...], preferred_element_type=F32)
        tag_b = tag[b * rows_b : (b + 1) * rows_b]
        for p in range(PARTS):
            prev = jnp.zeros((rows_b, part), F32)
            for c in range(CLU_DEV):
                row = coarse_ref[pl.ds(c, 1), pl.ds(p * part, part)].astype(F32)
                prev = jnp.where(tag_b == c + 1.0, row, prev)
            resid[pl.ds(b * rows_b, rows_b), pl.ds(p * part, part)] = (
                flat[p * rows_b : (p + 1) * rows_b] - prev
            ).astype(BF16)

    prod = lax.dot_general(
        resid[...], fines[...], (((1,), (1,)), ((), ())), preferred_element_type=F32
    )
    logits = (prod - 0.5 * fsq) * scale
    cluster_of = (iota((1, group_fines), 1) >> 6).astype(F32) + 1.0
    logits = jnp.where(cluster_of == tag, logits, -1e30)
    top = jnp.max(logits, axis=1, keepdims=True)
    expo = jnp.exp(logits - top)
    valid = jnp.where(tag > 0.0, 1.0, 0.0)
    probs = expo / jnp.sum(expo, axis=1, keepdims=True) * valid

    tot_box[z] = jnp.sum(probs, axis=0, keepdims=True)
    z_peers(
        lambda to: send(tot_box.at[z], tot_box.at[z], st_send.at[0], st_recv.at[0], own=to)
    )

    weights = jnp.transpose(probs).astype(BF16)

    def chunk_stats(to):
        at = pl.multiple_of(to * cols, 128)
        return jnp.dot(weights, resid[:, pl.ds(at, cols)], preferred_element_type=F32)

    steps = (n_z // 2, n_z - 1 - n_z // 2)
    sub = group_fines // SUBS

    def target_of(way, t):
        off = steps[0] - t if way == 0 else n_z - steps[1] + t
        return lax.rem(z + off, n_z)

    def ring_send(way, t, s, src):
        to = lax.rem(z + (1 if way == 0 else n_z - 1), n_z)
        send(
            src,
            rs_buf.at[way, t, pl.ds(s * sub, sub)],
            rs_send.at[way, t, s],
            rs_recv.at[way, t, s],
            own=to,
        )

    def ring_first():
        for way in range(2):
            if steps[way] > 0:
                rs_src[way] = chunk_stats(target_of(way, 0)).astype(BF16)
                for s in range(SUBS):
                    ring_send(way, 0, s, rs_src.at[way, pl.ds(s * sub, sub)])

    def ring_step(t):
        for s in range(SUBS):
            for way in range(2):
                if t >= steps[way]:
                    continue
                held = rs_buf.at[way, t - 1, pl.ds(s * sub, sub)]
                drain(held, rs_recv.at[way, t - 1, s])
                add = stats[target_of(way, t), pl.ds(s * sub, sub), :]
                held[...] = (held[...].astype(F32) + add).astype(BF16)
                ring_send(way, t, s, held)

    ring_first()

    @pl.loop(0, n_z)
    def _(to):
        stats[to] = chunk_stats(to)

    ring_step(1)

    if n_z > 1:
        drain(tot_box.at[pl.ds(0, n_z - 1)], st_recv.at[0])
    totals = tot_box[0]
    for k in range(1, n_z):
        totals = totals + tot_box[k]
    tot_out[...] = totals
    tot_col = jnp.sum(jnp.where(eye_f, totals, 0.0), axis=1, keepdims=True)
    share = 1.0 / (4.0 + tot_col)
    mean_share = share * (1.0 / FINE_PER)

    def put(ref, value):
        for h in range(n_h):
            ref[pl.ds(h * CLU_DEV, CLU_DEV), :] = value[:, h * 128 : (h + 1) * 128]

    def cluster_sum(value):
        return jnp.sum(value.reshape(CLU_DEV, FINE_PER, cols), axis=1)

    @pl.loop(0, n_z)
    def _(to):
        put(cpart.at[to], cluster_sum(stats[to] * mean_share))

    cbox[z] = cpart[z]
    z_peers(
        lambda to: send(cpart.at[to], cbox.at[z], st_send.at[1], st_recv.at[1], own=to)
    )
    my_cols = pl.ds(pl.multiple_of(z * cols, 128), cols)
    fine_part = fines[:, my_cols].astype(F32)
    put(
        own_piece,
        coarse_ref[:, my_cols].astype(F32) + cluster_sum(4.0 * fine_part * mean_share),
    )
    ring_step(2)

    if n_z > 1:
        drain(cbox.at[pl.ds(0, n_z - 1)], st_recv.at[1])
    piece = own_piece[...]
    for k in range(n_z):
        piece = piece + cbox[k]
    zbox[z] = piece
    z_peers(
        lambda to: send(zbox.at[z], zbox.at[z], st_send.at[2], st_recv.at[2], own=to)
    )
    ring_step(3)

    if n_z > 1:
        drain(zbox.at[pl.ds(0, n_z - 1)], st_recv.at[2])
    for k in range(n_z):
        got = zbox[k]
        for h in range(n_h):
            at = k * cols + h * 128
            block[pl.ds(at // part * CLU_DEV, CLU_DEV), pl.ds(at % part, 128)] = got[
                h * CLU_DEV : (h + 1) * CLU_DEV
            ]
    agbuf[core, y] = block[...].astype(BF16)

    @pl.loop(1, n_y)
    def _(k):
        dest = (x * n_y + lax.rem(y + k, n_y)) * 2 + core
        send(agbuf.at[core, y], agbuf.at[core, y], st_send.at[3], st_recv.at[3], dp=dest)

    ring_step(4)
    if n_y > 1:
        drain(agbuf.at[0, pl.ds(0, n_y - 1)], st_recv.at[3])
    other = me + 1 - 2 * core
    send(agbuf.at[core], agbuf.at[core], st_send.at[4], st_recv.at[4], dp=other)
    ring_step(5)
    drain(agbuf.at[0], st_recv.at[4])
    rows_x = 2 * n_y * CLU_DEV
    within_y = lax.div(within, 2 * CLU_DEV)
    within_core = (within >> 2) & 1
    from_row = (within_core * n_y + within_y) * BLK + quarter * CAP + (within & 3)
    perm_x = (in_row == from_row).astype(F32).astype(BF16)
    gathered = jnp.dot(
        perm_x, agbuf[...].reshape(2 * n_y * BLK, part), preferred_element_type=F32
    ).astype(BF16)
    own_rows = pl.ds(pl.multiple_of(x * rows_x, rows_x), rows_x)
    for p in range(PARTS):
        coarse_out[own_rows, pl.ds(p * part, part)] = gathered[p * rows_x : (p + 1) * rows_x]
    half_cols = pl.ds(pl.multiple_of(core * (width // 2), 128), width // 2)
    mine_x = coarse_out.at[own_rows, half_cols]

    @pl.loop(1, n_x)
    def _(k):
        dest = (lax.rem(x + k, n_x) * n_y + y) * 2 + core
        send(mine_x, mine_x, st_send.at[5], st_recv.at[5], dp=dest)

    ring_step(6)
    others = coarse_out.at[pl.ds(0, rows_x * (n_x - 1)), pl.ds(0, width // 2)]
    drain(others, st_recv.at[5])

    @pl.loop(1, n_x)
    def _(k):
        at_rows = pl.ds(pl.multiple_of(lax.rem(x + k, n_x) * rows_x, rows_x), rows_x)
        view = coarse_out.at[at_rows, half_cols]
        send(view, view, st_send.at[6], st_recv.at[6], dp=other)

    for t in range(7, steps[0]):
        ring_step(t)

    sums = stats[z]
    for way in range(2):
        if steps[way] > 0:
            for s in range(SUBS):
                last = steps[way] - 1
                drain(rs_buf.at[way, last, pl.ds(s * sub, sub)], rs_recv.at[way, last, s])
            sums = sums + rs_buf[way, steps[way] - 1].astype(F32)
    fine_out[...] = (4.0 * fine_part + sums) * share

    drain(others, st_recv.at[6])
    drain(ids_box.at[pl.ds(0, n_dp - 1)], ids_send)
    drain(outbox.at[pl.ds(0, (n_dp - 1) * BLK)], a2a_send)
    if n_z > 1:
        drain(tot_box.at[pl.ds(0, n_z - 1)], st_send.at[0])
        drain(cbox.at[pl.ds(0, n_z - 1)], st_send.at[1])
        drain(zbox.at[pl.ds(0, n_z - 1)], st_send.at[2])
    if n_y > 1:
        drain(agbuf.at[0, pl.ds(0, n_y - 1)], st_send.at[3])
    drain(agbuf.at[0], st_send.at[4])
    drain(others, st_send.at[5])
    drain(others, st_send.at[6])
    for way in range(2):
        for t in range(steps[way]):
            for s in range(SUBS):
                drain(rs_buf.at[way, t, pl.ds(s * sub, sub)], rs_send.at[way, t, s])


def solution(mesh):
    n_dp, n_z = mesh.shape["dp"], mesh.shape["own"]
    n_x = N_X
    n_y = n_dp // (2 * n_x)

    def on_device(embeddings, coarse_ids, fine_cents, coarse_prev):
        rows, width = embeddings.shape
        group_fines = fine_cents.shape[0]
        cols = width // n_z
        part = width // PARTS
        lanes = cols // 128 * CLU_DEV
        vmem = pl.BlockSpec(memory_space=pltpu.VMEM)
        hbm = pl.BlockSpec(memory_space=pl.ANY)
        dma = pltpu.SemaphoreType.DMA
        fine_next, totals, coarse_next = pl.pallas_call(
            functools.partial(kernel, n_x, n_y, n_z),
            out_shape=(
                jax.ShapeDtypeStruct((group_fines, cols), F32),
                jax.ShapeDtypeStruct((1, group_fines), F32),
                jax.ShapeDtypeStruct((n_dp * CLU_DEV, width), BF16),
            ),
            in_specs=[hbm, vmem, hbm, vmem],
            out_specs=(vmem, vmem, vmem),
            scratch_shapes=[
                pltpu.VMEM((PARTS * rows, part), BF16),
                pltpu.VMEM((group_fines, width), BF16),
                pltpu.VMEM((n_dp * BLK, part), BF16),
                pltpu.VMEM((n_dp * BLK, part), BF16),
                pltpu.VMEM((n_dp, 1, rows), jnp.int32),
                pltpu.VMEM((n_dp, rows), F32),
                pltpu.VMEM((n_dp * CAP, width), BF16),
                pltpu.VMEM((n_z, group_fines, cols), F32),
                pltpu.VMEM((2, group_fines, cols), BF16),
                pltpu.VMEM((2, max(n_z // 2, 1), group_fines, cols), BF16),
                pltpu.VMEM((n_z, 1, group_fines), F32),
                pltpu.VMEM((n_z, lanes, 128), F32),
                pltpu.VMEM((n_z, lanes, 128), F32),
                pltpu.VMEM((n_z, lanes, 128), F32),
                pltpu.VMEM((lanes, 128), F32),
                pltpu.VMEM((BLK, part), F32),
                pltpu.VMEM((2, n_y, BLK, part), BF16),
                dma((PARTS + 1,)),
                dma(()),
                dma(()),
                dma(()),
                dma((n_x,)),
                dma((2, max(n_z // 2, 1), SUBS)),
                dma((2, max(n_z // 2, 1), SUBS)),
                dma((7,)),
                dma((7,)),
            ],
            compiler_params=pltpu.CompilerParams(
                collective_id=0, has_side_effects=True, vmem_limit_bytes=48 * 2**20
            ),
        )(embeddings, coarse_ids.reshape(1, 1, rows), fine_cents, coarse_prev)
        return fine_next, totals.reshape(group_fines), coarse_next

    placed = (P(("dp", "own"), None), P(("dp", "own")), P("dp", None), P("dp", None))
    return jax.shard_map(
        on_device,
        mesh=mesh,
        in_specs=placed,
        out_specs=(P("dp", "own"), P("dp"), P()),
        check_vma=False,
    )
```

```python
import functools
import math

import jax
import jax.numpy as jnp
from jax import lax
from jax.experimental import pallas as pl
from jax.experimental.pallas import tpu as pltpu
from jax.sharding import PartitionSpec as P

MESH = pl.DeviceIdType.MESH
FINE_PER = 64
CLU_DEV = 4
CAP = 4
PARTS = 4
BLK = CAP * PARTS
N_X = 4
SUBS = 2
F32 = jnp.float32
BF16 = jnp.bfloat16


def drain(ref, sem):
    pltpu.make_async_copy(ref, ref, sem).wait()


def iota(shape, dim):
    return lax.broadcasted_iota(jnp.int32, shape, dim)


def kernel(
    n_x,
    n_y,
    n_z,
    emb_hbm,
    ids_hbm,
    fines_hbm,
    coarse_hbm,
    fine_hbm,
    tot_hbm,
    blocks_hbm,
    emb,
    ids_ref,
    fines,
    coarse_ref,
    outbox,
    inbox,
    ids_box,
    ids_f,
    resid,
    prod_box,
    stats,
    rs_src,
    rs_buf,
    tot_box,
    cpart,
    cbox,
    folded,
    mine_y,
    gath,
    fine_out,
    tot_out,
    load_sem,
    ids_send,
    ids_recv,
    a2a_send,
    a2a_recv,
    rs_send,
    rs_recv,
    st_send,
    st_recv,
    y_recv,
    x_recv,
    core_recv,
    store_sem,
):
    n_dp = 2 * n_x * n_y
    rows, width = emb_hbm.shape
    part = width // PARTS
    group_fines = fines.shape[0]
    cols = width // n_z
    scale = 4.0 / math.sqrt(width)

    me = lax.axis_index("dp")
    z = lax.axis_index("own")
    core = lax.rem(me, 2)
    chip = lax.div(me, 2)
    y = lax.rem(chip, n_y)
    x = lax.div(chip, n_y)

    def send(src, dst, send_sem, recv_sem, **to):
        copy = pltpu.make_async_remote_copy(
            src_ref=src,
            dst_ref=dst,
            send_sem=send_sem,
            recv_sem=recv_sem,
            device_id=to,
            device_id_type=MESH,
        )
        copy.start()

    def z_peers(body):
        @pl.loop(1, n_z)
        def _(k):
            body(lax.rem(z + k, n_z))

    barrier = pltpu.get_barrier_semaphore()

    loads = []
    for p in range(PARTS):
        loads.append(
            pltpu.make_async_copy(
                emb_hbm.at[:, pl.ds(p * part, part)],
                emb.at[pl.ds(p * rows, rows)],
                load_sem.at[p],
            )
        )
    loads.append(pltpu.make_async_copy(fines_hbm, fines, load_sem.at[PARTS]))
    loads.append(pltpu.make_async_copy(coarse_hbm, coarse_ref, load_sem.at[PARTS + 1]))
    load_ids = pltpu.make_async_copy(ids_hbm, ids_ref, load_sem.at[PARTS + 2])
    load_ids.start()
    for load in loads:
        load.start()

    @pl.loop(1, n_dp)
    def _(k):
        pl.semaphore_signal(
            barrier, inc=1, device_id={"dp": lax.rem(me + k, n_dp)}, device_id_type=MESH
        )

    @pl.loop(1, n_z)
    def _(k):
        pl.semaphore_signal(
            barrier, inc=1, device_id={"own": lax.rem(z + k, n_z)}, device_id_type=MESH
        )

    load_ids.wait()
    ids = ids_ref[0]
    owner = ids >> 2
    owner_rows = jnp.broadcast_to(owner.astype(F32), (rows, rows))
    eye = iota((rows, rows), 0) == iota((rows, rows), 1)
    before = iota((rows, rows), 0) < iota((rows, rows), 1)
    owner_col = jnp.sum(jnp.where(eye, owner_rows, 0.0), axis=1, keepdims=True)
    same = jnp.where(before & (owner_col == owner_rows), 1.0, 0.0)
    rank = jnp.sum(same, axis=0, keepdims=True).astype(jnp.int32)
    y_bits = n_y.bit_length() - 1
    to_core = owner & 1
    to_y = (owner >> 1) & (n_y - 1)
    to_x = owner >> (1 + y_bits)
    dxi = (to_x - x + 2 * n_x - 1) & (n_x - 1)
    dy = (to_y - y + n_y) & (n_y - 1)
    half = n_y // 2
    dyi = jnp.where(dy >= half, 2 * (dy - half), 2 * (half - dy) - 1)
    place = ((to_core * n_x + dxi) * n_y + dyi) * BLK + rank
    target = jnp.concatenate([place + p * CAP for p in range(PARTS)], axis=1)

    ids_box[n_dp - 2] = ids
    for load in loads[:PARTS]:
        load.wait()
    pl.semaphore_wait(barrier, n_dp - 1 + n_z - 1)

    chunk = n_y * BLK

    @pl.loop(0, 2 * n_x)
    def _(jc):
        base = pl.multiple_of(jc * chunk, chunk)
        hot = (iota((chunk, PARTS * rows), 0) + base == target).astype(F32).astype(BF16)
        outbox[pl.ds(base, chunk), :] = jnp.dot(
            hot, emb[...], preferred_element_type=F32
        ).astype(BF16)
        dest_core = lax.div(jc, n_x)
        at_x = lax.rem(jc, n_x)
        dest_x = lax.rem(x + at_x + 1, n_x)
        flip = lax.rem(dest_core + core, 2)
        for at_y in range(n_y):
            step = (at_y + 1) // 2
            delta = (n_y // 2 + (step if at_y % 2 == 0 else -step)) % n_y
            dest = (dest_x * n_y + lax.rem(y + delta, n_y)) * 2 + dest_core
            slot = (at_x * n_y + at_y) * 2 + flip
            src = outbox.at[pl.ds(pl.multiple_of(base + at_y * BLK, BLK), BLK)]
            dst = inbox.at[pl.ds(pl.multiple_of(slot * BLK, BLK), BLK)]

            def post():
                send(ids_ref.at[0], ids_box.at[slot], ids_send, ids_recv, dp=dest)
                send(src, dst, a2a_send, a2a_recv.at[at_x], dp=dest)

            if at_y < n_y - 1:
                post()
            else:
                mine = (at_x == n_x - 1) & (flip == 0)
                pl.when(jnp.logical_not(mine))(post)

                @pl.when(mine)
                def _():
                    pltpu.make_async_copy(src, dst, a2a_recv.at[at_x]).start()

    loads[PARTS].wait()
    loads[PARTS + 1].wait()
    fsq_col = jnp.sum(jnp.square(fines[...].astype(F32)), axis=1, keepdims=True)
    eye_f = iota((group_fines, group_fines), 0) == iota((group_fines, group_fines), 1)
    fsq = jnp.sum(jnp.where(eye_f, fsq_col, 0.0), axis=0, keepdims=True)

    drain(ids_box.at[pl.ds(0, n_dp - 1)], ids_recv)
    for i in range(n_dp):
        ids_f[pl.ds(i, 1), :] = ids_box[i].astype(F32)
    slots = n_dp * CAP
    spread = (iota((slots, n_dp), 0) >> 2) == iota((slots, n_dp), 1)
    seen = jnp.dot(
        spread.astype(F32).astype(BF16), ids_f[...].astype(BF16), preferred_element_type=F32
    )
    low = (me * CLU_DEV).astype(F32)
    ours = jnp.where((seen >= low) & (seen < low + CLU_DEV), 1.0, 0.0)
    order = jnp.dot(
        ours.astype(BF16), before.astype(F32).astype(BF16), preferred_element_type=F32
    )
    nth = (iota((slots, rows), 0) & (CAP - 1)).astype(F32)
    tag = jnp.sum(
        jnp.where(order == nth, ours * (seen - low + 1.0), 0.0), axis=1, keepdims=True
    )

    src_b = 2 * n_y
    rows_b = src_b * CAP
    out_row = iota((src_b * BLK, src_b * BLK), 0)
    in_row = iota((src_b * BLK, src_b * BLK), 1)
    quarter = lax.div(out_row, rows_b)
    within = lax.rem(out_row, rows_b)
    perm = (in_row == (within >> 2) * BLK + quarter * CAP + (within & 3)).astype(F32).astype(BF16)
    for b in range(n_x):
        arrived = inbox.at[pl.ds(b * src_b * BLK, src_b * BLK)]
        drain(arrived, a2a_recv.at[b])
        flat = jnp.dot(perm, arrived[...], preferred_element_type=F32)
        tag_b = tag[b * rows_b : (b + 1) * rows_b]
        for p in range(PARTS):
            prev = jnp.zeros((rows_b, part), F32)
            for c in range(CLU_DEV):
                row = coarse_ref[pl.ds(c, 1), pl.ds(p * part, part)].astype(F32)
                prev = jnp.where(tag_b == c + 1.0, row, prev)
            resid[pl.ds(b * rows_b, rows_b), pl.ds(p * part, part)] = (
                flat[p * rows_b : (p + 1) * rows_b] - prev
            ).astype(BF16)
        prod_box[pl.ds(b * rows_b, rows_b), :] = lax.dot_general(
            resid[pl.ds(b * rows_b, rows_b), :],
            fines[...],
            (((1,), (1,)), ((), ())),
            preferred_element_type=F32,
        )

    prod = prod_box[...]
    logits = (prod - 0.5 * fsq) * scale
    cluster_of = (iota((1, group_fines), 1) >> 6).astype(F32) + 1.0
    logits = jnp.where(cluster_of == tag, logits, -1e30)
    top = jnp.max(logits, axis=1, keepdims=True)
    expo = jnp.exp(logits - top)
    valid = jnp.where(tag > 0.0, 1.0, 0.0)
    probs = expo / jnp.sum(expo, axis=1, keepdims=True) * valid

    tot_box[z] = jnp.sum(probs, axis=0, keepdims=True)
    z_peers(
        lambda to: send(tot_box.at[z], tot_box.at[z], st_send.at[0], st_recv.at[0], own=to)
    )

    weights = jnp.transpose(probs).astype(BF16)

    def chunk_stats(to):
        at = pl.multiple_of(to * cols, 128)
        return jnp.dot(weights, resid[:, pl.ds(at, cols)], preferred_element_type=F32)

    steps = (n_z // 2, n_z - 1 - n_z // 2)
    sub = group_fines // SUBS

    def target_of(way, t):
        off = steps[0] - t if way == 0 else n_z - steps[1] + t
        return lax.rem(z + off, n_z)

    def ring_send(way, t, s, src):
        to = lax.rem(z + (1 if way == 0 else n_z - 1), n_z)
        send(
            src,
            rs_buf.at[way, t, pl.ds(s * sub, sub)],
            rs_send.at[way, t, s],
            rs_recv.at[way, t, s],
            own=to,
        )

    def ring_first():
        for way in range(2):
            if steps[way] > 0:
                rs_src[way] = chunk_stats(target_of(way, 0)).astype(BF16)
                for s in range(SUBS):
                    ring_send(way, 0, s, rs_src.at[way, pl.ds(s * sub, sub)])

    def ring_step(t):
        for s in range(SUBS):
            for way in range(2):
                if t >= steps[way]:
                    continue
                held = rs_buf.at[way, t - 1, pl.ds(s * sub, sub)]
                drain(held, rs_recv.at[way, t - 1, s])
                add = stats[target_of(way, t), pl.ds(s * sub, sub), :]
                held[...] = (held[...].astype(F32) + add).astype(BF16)
                ring_send(way, t, s, held)

    ring_first()
    wide = part // cols
    for p in range(PARTS):
        quarter_stats = jnp.dot(
            weights, resid[:, pl.ds(p * part, part)], preferred_element_type=F32
        )
        for k in range(wide):
            stats[p * wide + k] = quarter_stats[:, k * cols : (k + 1) * cols]
    ring_step(1)
    ring_step(2)

    drain(tot_box.at[pl.ds(0, n_z - 1)], st_recv.at[0])
    totals = tot_box[0]
    for k in range(1, n_z):
        totals = totals + tot_box[k]
    tot_out[...] = totals
    store_tot = pltpu.make_async_copy(tot_out, tot_hbm, store_sem.at[0])
    store_tot.start()
    tot_col = jnp.sum(jnp.where(eye_f, totals, 0.0), axis=1, keepdims=True)
    share = 1.0 / (4.0 + tot_col)
    mean_share = share * (1.0 / FINE_PER)

    def cluster_sum(value):
        return jnp.sum(value.reshape(CLU_DEV, FINE_PER, cols), axis=1)

    for p in range(PARTS):
        for k in range(wide):
            folded[pl.ds(k * CLU_DEV, CLU_DEV), :] = cluster_sum(stats[p * wide + k] * mean_share)
        cpart[p] = folded[...].astype(BF16)
    my_quarter = lax.rem(z, PARTS)
    cbox[z] = cpart[my_quarter]
    for d in range(1, n_z):
        to = lax.rem(z + d, n_z)
        send(cpart.at[lax.rem(to, PARTS)], cbox.at[z], st_send.at[1], st_recv.at[1], own=to)
    for k in range(wide):
        at = pl.ds(pl.multiple_of(my_quarter * part + k * cols, 128), cols)
        folded[pl.ds(k * CLU_DEV, CLU_DEV), :] = coarse_ref[:, at].astype(F32) + cluster_sum(
            4.0 * fines[:, at].astype(F32) * mean_share
        )
    ring_step(3)
    ring_step(4)

    drain(cbox.at[pl.ds(0, n_z - 1)], st_recv.at[1])
    piece = folded[...]
    for k in range(n_z):
        piece = piece + cbox[k].astype(F32)
    quarter_cols = pl.ds(pl.multiple_of(my_quarter * cols, 128), cols)
    mine = mine_y.at[:, quarter_cols]
    mine[...] = piece.astype(BF16)
    for d in (1, n_z - 1, n_z - 2):
        send(mine, mine, st_send.at[2], st_recv.at[2], own=lax.rem(z + d, n_z))
    ring_step(5)
    drain(mine_y.at[:, pl.ds(0, 3 * cols)], st_recv.at[2])

    other = me + 1 - 2 * core
    gath[core, x, y] = mine_y[...]
    near = sorted(range(1, n_y), key=lambda k: min(k, n_y - k))

    def along_x(at_y):
        block = gath.at[core, x, at_y]
        for k in range(1, n_x):
            dest = (lax.rem(x + k, n_x) * n_y + y) * 2 + core
            send(block, block, st_send.at[5], x_recv.at[k], dp=dest)

    for k in near:
        dest = (x * n_y + lax.rem(y + n_y - k, n_y)) * 2 + core
        block = gath.at[core, x, y]
        send(block, block, st_send.at[3], y_recv.at[k], dp=dest)
    along_x(y)
    ring_step(6)
    for k in near:
        at_y = lax.rem(y + k, n_y)
        drain(gath.at[core, x, at_y], y_recv.at[k])
        along_x(at_y)

    def pass_on(k):
        column = gath.at[core, lax.rem(x - k + n_x, n_x)]
        send(column, column, st_send.at[4], core_recv.at[k], dp=other)
        store_column(core, k, k)

    stores = []

    def store_column(of_core, k, sem):
        at = lax.rem(x - k + n_x, n_x)
        stores.append(
            pltpu.make_async_copy(
                gath.at[of_core, at], blocks_hbm.at[of_core, at], store_sem.at[2 + sem]
            )
        )
        stores[-1].start()

    pass_on(0)
    for t in range(7, steps[0]):
        ring_step(t)
    for k in range(1, n_x):
        drain(gath.at[core, lax.rem(x - k + n_x, n_x)], x_recv.at[k])
        pass_on(k)

    sums = stats[z]
    for way in range(2):
        if steps[way] > 0:
            for s in range(SUBS):
                last = steps[way] - 1
                drain(rs_buf.at[way, last, pl.ds(s * sub, sub)], rs_recv.at[way, last, s])
            sums = sums + rs_buf[way, steps[way] - 1].astype(F32)
    my_cols = pl.ds(pl.multiple_of(z * cols, 128), cols)
    fine_out[...] = (4.0 * fines[:, my_cols].astype(F32) + sums) * share

    store_fine = pltpu.make_async_copy(fine_out, fine_hbm, store_sem.at[1])
    store_fine.start()

    for k in range(n_x):
        at = lax.rem(x - k + n_x, n_x)
        drain(gath.at[1 - core, at], core_recv.at[k])
        store_column(1 - core, k, n_x + k)
    for store in [store_tot, store_fine, *stores]:
        store.wait()
    drain(ids_box.at[pl.ds(0, n_dp - 1)], ids_send)
    drain(outbox.at[pl.ds(0, (n_dp - 1) * BLK)], a2a_send)
    drain(tot_box.at[pl.ds(0, n_z - 1)], st_send.at[0])
    drain(cbox.at[pl.ds(0, n_z - 1)], st_send.at[1])
    drain(mine_y.at[:, pl.ds(0, 3 * cols)], st_send.at[2])
    drain(gath.at[0, 0, pl.ds(0, n_y - 1)], st_send.at[3])
    drain(gath.at[0], st_send.at[4])
    drain(gath.at[0, pl.ds(0, n_x - 1)], st_send.at[5])
    for way in range(2):
        for t in range(steps[way]):
            for s in range(SUBS):
                drain(rs_buf.at[way, t, pl.ds(s * sub, sub)], rs_send.at[way, t, s])


def arrange(n_y, blocks, fine, tot, fine_out, tot_out, coarse_out):
    blk, width = blocks.shape[-2:]
    wide = blk // CLU_DEV
    cols = width // PARTS
    rows_x = 2 * n_y * CLU_DEV
    out_row = iota((rows_x * wide, rows_x * wide), 0)
    in_row = iota((rows_x * wide, rows_x * wide), 1)
    within = lax.rem(out_row, rows_x)
    from_block = ((within >> 2) & 1) * n_y + lax.div(within, 2 * CLU_DEV)
    from_row = from_block * blk + lax.div(out_row, rows_x) * CLU_DEV + (within & 3)
    perm = (in_row == from_row).astype(F32).astype(BF16)
    both = jnp.concatenate([blocks[c, 0, i] for c in range(2) for i in range(n_y)], axis=0)
    rows = jnp.dot(perm, both, preferred_element_type=F32).astype(BF16)
    for p in range(PARTS):
        for j in range(wide):
            coarse_out[:, pl.ds((p * wide + j) * cols, cols)] = rows[
                j * rows_x : (j + 1) * rows_x, p * cols : (p + 1) * cols
            ]
    fine_out[...] = fine[...]
    tot_out[...] = tot[...]


def solution(mesh):
    n_dp, n_z = mesh.shape["dp"], mesh.shape["own"]
    n_x = N_X
    n_y = n_dp // (2 * n_x)

    def on_device(embeddings, coarse_ids, fine_cents, coarse_prev):
        rows, width = embeddings.shape
        group_fines = fine_cents.shape[0]
        cols = width // n_z
        part = width // PARTS
        blk = part // cols * CLU_DEV
        hbm = pl.BlockSpec(memory_space=pl.ANY)
        dma = pltpu.SemaphoreType.DMA
        fine_next, totals, blocks = pl.pallas_call(
            functools.partial(kernel, n_x, n_y, n_z),
            out_shape=(
                jax.ShapeDtypeStruct((group_fines, cols), F32),
                jax.ShapeDtypeStruct((1, group_fines), F32),
                jax.ShapeDtypeStruct((2, n_x, n_y, blk, PARTS * cols), BF16),
            ),
            in_specs=[hbm, hbm, hbm, hbm],
            out_specs=(hbm, hbm, hbm),
            scratch_shapes=[
                pltpu.VMEM((PARTS * rows, part), BF16),
                pltpu.VMEM((1, 1, rows), jnp.int32),
                pltpu.VMEM((group_fines, width), BF16),
                pltpu.VMEM((CLU_DEV, width), BF16),
                pltpu.VMEM((n_dp * BLK, part), BF16),
                pltpu.VMEM((n_dp * BLK, part), BF16),
                pltpu.VMEM((n_dp, 1, rows), jnp.int32),
                pltpu.VMEM((n_dp, rows), F32),
                pltpu.VMEM((n_dp * CAP, width), BF16),
                pltpu.VMEM((n_dp * CAP, group_fines), F32),
                pltpu.VMEM((n_z, group_fines, cols), F32),
                pltpu.VMEM((2, group_fines, cols), BF16),
                pltpu.VMEM((2, max(n_z // 2, 1), group_fines, cols), BF16),
                pltpu.VMEM((n_z, 1, group_fines), F32),
                pltpu.VMEM((PARTS, blk, cols), BF16),
                pltpu.VMEM((n_z, blk, cols), BF16),
                pltpu.VMEM((blk, cols), F32),
                pltpu.VMEM((blk, PARTS * cols), BF16),
                pltpu.VMEM((2, n_x, n_y, blk, PARTS * cols), BF16),
                pltpu.VMEM((group_fines, cols), F32),
                pltpu.VMEM((1, group_fines), F32),
                dma((PARTS + 3,)),
                dma(()),
                dma(()),
                dma(()),
                dma((n_x,)),
                dma((2, max(n_z // 2, 1), SUBS)),
                dma((2, max(n_z // 2, 1), SUBS)),
                dma((6,)),
                dma((3,)),
                dma((n_y,)),
                dma((n_x,)),
                dma((n_x,)),
                dma((2 + 2 * n_x,)),
            ],
            compiler_params=pltpu.CompilerParams(
                collective_id=0, has_side_effects=True, vmem_limit_bytes=60 * 2**20
            ),
        )(embeddings, coarse_ids.reshape(1, 1, rows), fine_cents, coarse_prev)
        whole_fine = pl.BlockSpec((group_fines, cols), lambda i: (0, 0))
        whole_tot = pl.BlockSpec((1, group_fines), lambda i: (0, 0))
        fine_next, totals, coarse_next = pl.pallas_call(
            functools.partial(arrange, n_y),
            grid=(n_x,),
            out_shape=(
                jax.ShapeDtypeStruct((group_fines, cols), F32),
                jax.ShapeDtypeStruct((1, group_fines), F32),
                jax.ShapeDtypeStruct((n_dp * CLU_DEV, width), BF16),
            ),
            in_specs=[
                pl.BlockSpec((2, 1, n_y, blk, PARTS * cols), lambda i: (0, i, 0, 0, 0)),
                whole_fine,
                whole_tot,
            ],
            out_specs=(
                whole_fine,
                whole_tot,
                pl.BlockSpec((2 * n_y * CLU_DEV, width), lambda i: (i, 0)),
            ),
            compiler_params=pltpu.CompilerParams(vmem_limit_bytes=60 * 2**20),
        )(blocks, fine_next, totals)
        return fine_next, totals.reshape(group_fines), coarse_next

    placed = (P(("dp", "own"), None), P(("dp", "own")), P("dp", None), P("dp", None))
    return jax.shard_map(
        on_device,
        mesh=mesh,
        in_specs=placed,
        out_specs=(P("dp", "own"), P("dp"), P()),
        check_vma=False,
    )
```

```python
import functools
import math

import jax
import jax.numpy as jnp
from jax import lax
from jax.experimental import pallas as pl
from jax.experimental.pallas import tpu as pltpu
from jax.sharding import PartitionSpec as P

MESH = pl.DeviceIdType.MESH
FINE_PER = 64
CLU_DEV = 4
CAP = 4
PARTS = 4
BLK = CAP * PARTS
N_X = 4
SUBS = 4
F32 = jnp.float32
BF16 = jnp.bfloat16


def drain(ref, sem):
    pltpu.make_async_copy(ref, ref, sem).wait()


def iota(shape, dim):
    return lax.broadcasted_iota(jnp.int32, shape, dim)


def kernel(
    n_x,
    n_y,
    n_z,
    emb_hbm,
    ids_hbm,
    fines_hbm,
    coarse_hbm,
    fine_out,
    tot_out,
    coarse_out,
    emb,
    ids_ref,
    fines,
    coarse_ref,
    outbox,
    inbox,
    ids_box,
    ids_f,
    resid,
    prod_box,
    stats,
    rs_src,
    rs_buf,
    tot_box,
    cpart,
    cbox,
    folded,
    gath,
    load_sem,
    ids_send,
    ids_recv,
    a2a_send,
    a2a_recv,
    rs_send,
    rs_recv,
    st_send,
    st_recv,
    y_recv,
    x_recv,
    core_recv,
):
    n_dp = 2 * n_x * n_y
    rows, width = emb_hbm.shape
    part = width // PARTS
    group_fines = fines.shape[0]
    cols = width // n_z
    scale = 4.0 / math.sqrt(width)

    me = lax.axis_index("dp")
    z = lax.axis_index("own")
    core = lax.rem(me, 2)
    chip = lax.div(me, 2)
    y = lax.rem(chip, n_y)
    x = lax.div(chip, n_y)

    def send(src, dst, send_sem, recv_sem, **to):
        copy = pltpu.make_async_remote_copy(
            src_ref=src,
            dst_ref=dst,
            send_sem=send_sem,
            recv_sem=recv_sem,
            device_id=to,
            device_id_type=MESH,
        )
        copy.start()

    def far_first(n):
        return sorted(range(1, n), key=lambda k: -min(k, n - k))

    barrier = pltpu.get_barrier_semaphore()

    loads = []
    for p in range(PARTS):
        loads.append(
            pltpu.make_async_copy(
                emb_hbm.at[:, pl.ds(p * part, part)],
                emb.at[pl.ds(p * rows, rows)],
                load_sem.at[p],
            )
        )
    loads.append(pltpu.make_async_copy(fines_hbm, fines, load_sem.at[PARTS]))
    loads.append(pltpu.make_async_copy(coarse_hbm, coarse_ref, load_sem.at[PARTS + 1]))
    load_ids = pltpu.make_async_copy(ids_hbm, ids_ref, load_sem.at[PARTS + 2])
    load_ids.start()
    for load in loads:
        load.start()

    @pl.loop(1, n_dp)
    def _(k):
        pl.semaphore_signal(
            barrier, inc=1, device_id={"dp": lax.rem(me + k, n_dp)}, device_id_type=MESH
        )

    @pl.loop(1, n_z)
    def _(k):
        pl.semaphore_signal(
            barrier, inc=1, device_id={"own": lax.rem(z + k, n_z)}, device_id_type=MESH
        )

    quarter_from = (1, n_z - 1, 2)
    quarter_to = (n_z - 1, 1, n_z - 2)

    @pl.loop(1, n_y)
    def _(k):
        dest = (x * n_y + lax.rem(y + k, n_y)) * 2 + core
        for d in quarter_from:
            pl.semaphore_signal(
                barrier,
                inc=1,
                device_id={"dp": dest, "own": lax.rem(z + d, n_z)},
                device_id_type=MESH,
            )

    load_ids.wait()
    ids = ids_ref[0]
    owner = ids >> 2
    owner_rows = jnp.broadcast_to(owner.astype(F32), (rows, rows))
    eye = iota((rows, rows), 0) == iota((rows, rows), 1)
    before = iota((rows, rows), 0) < iota((rows, rows), 1)
    owner_col = jnp.sum(jnp.where(eye, owner_rows, 0.0), axis=1, keepdims=True)
    same = jnp.where(before & (owner_col == owner_rows), 1.0, 0.0)
    rank = jnp.sum(same, axis=0, keepdims=True).astype(jnp.int32)
    y_bits = n_y.bit_length() - 1
    to_core = owner & 1
    to_y = (owner >> 1) & (n_y - 1)
    to_x = owner >> (1 + y_bits)
    dxi = (to_x - x + 2 * n_x - 1) & (n_x - 1)
    dy = (to_y - y + n_y) & (n_y - 1)
    half = n_y // 2
    dyi = jnp.where(dy >= half, 2 * (dy - half), 2 * (half - dy) - 1)
    place = ((to_core * n_x + dxi) * n_y + dyi) * BLK + rank
    target = jnp.concatenate([place + p * CAP for p in range(PARTS)], axis=1)

    ids_box[n_dp - 2] = ids
    for load in loads[:PARTS]:
        load.wait()
    chunk = n_y * BLK

    def build(jc):
        base = pl.multiple_of(jc * chunk, chunk)
        hot = (iota((chunk, PARTS * rows), 0) + base == target).astype(F32).astype(BF16)
        outbox[pl.ds(base, chunk), :] = jnp.dot(
            hot, emb[...], preferred_element_type=F32
        ).astype(BF16)

    build(0)
    pl.semaphore_wait(barrier, n_dp - 1 + n_z - 1 + 3 * (n_y - 1))

    @pl.loop(0, 2 * n_x)
    def _(jc):
        base = pl.multiple_of(jc * chunk, chunk)
        dest_core = lax.div(jc, n_x)
        at_x = lax.rem(jc, n_x)
        dest_x = lax.rem(x + at_x + 1, n_x)
        flip = lax.rem(dest_core + core, 2)
        for at_y in range(n_y):
            step = (at_y + 1) // 2
            delta = (n_y // 2 + (step if at_y % 2 == 0 else -step)) % n_y
            dest = (dest_x * n_y + lax.rem(y + delta, n_y)) * 2 + dest_core
            slot = (at_x * n_y + at_y) * 2 + flip
            src = outbox.at[pl.ds(pl.multiple_of(base + at_y * BLK, BLK), BLK)]
            dst = inbox.at[pl.ds(pl.multiple_of(slot * BLK, BLK), BLK)]

            def post():
                send(ids_ref.at[0], ids_box.at[slot], ids_send, ids_recv, dp=dest)
                send(src, dst, a2a_send, a2a_recv.at[at_x], dp=dest)

            if at_y < n_y - 1:
                post()
            else:
                mine = (at_x == n_x - 1) & (flip == 0)
                pl.when(jnp.logical_not(mine))(post)

                @pl.when(mine)
                def _():
                    pltpu.make_async_copy(src, dst, a2a_recv.at[at_x]).start()

        @pl.when(jc + 1 < 2 * n_x)
        def _():
            build(jc + 1)

    loads[PARTS].wait()
    loads[PARTS + 1].wait()
    fsq_col = jnp.sum(jnp.square(fines[...].astype(F32)), axis=1, keepdims=True)
    eye_f = iota((group_fines, group_fines), 0) == iota((group_fines, group_fines), 1)
    fsq = jnp.sum(jnp.where(eye_f, fsq_col, 0.0), axis=0, keepdims=True)

    drain(ids_box.at[pl.ds(0, n_dp - 1)], ids_recv)
    for i in range(n_dp):
        ids_f[pl.ds(i, 1), :] = ids_box[i].astype(F32)
    slots = n_dp * CAP
    spread = (iota((slots, n_dp), 0) >> 2) == iota((slots, n_dp), 1)
    seen = jnp.dot(
        spread.astype(F32).astype(BF16), ids_f[...].astype(BF16), preferred_element_type=F32
    )
    low = (me * CLU_DEV).astype(F32)
    ours = jnp.where((seen >= low) & (seen < low + CLU_DEV), 1.0, 0.0)
    order = jnp.dot(
        ours.astype(BF16), before.astype(F32).astype(BF16), preferred_element_type=F32
    )
    nth = (iota((slots, rows), 0) & (CAP - 1)).astype(F32)
    tag = jnp.sum(
        jnp.where(order == nth, ours * (seen - low + 1.0), 0.0), axis=1, keepdims=True
    )

    src_b = 2 * n_y
    rows_b = src_b * CAP
    out_row = iota((src_b * BLK, src_b * BLK), 0)
    in_row = iota((src_b * BLK, src_b * BLK), 1)
    quarter = out_row >> (rows_b.bit_length() - 1)
    within = out_row & (rows_b - 1)
    perm = (in_row == (within >> 2) * BLK + quarter * CAP + (within & 3)).astype(F32).astype(BF16)
    for b in range(n_x):
        arrived = inbox.at[pl.ds(b * src_b * BLK, src_b * BLK)]
        drain(arrived, a2a_recv.at[b])
        flat = jnp.dot(perm, arrived[...], preferred_element_type=F32)
        tag_b = tag[b * rows_b : (b + 1) * rows_b]
        for p in range(PARTS):
            prev = jnp.zeros((rows_b, part), F32)
            for c in range(CLU_DEV):
                row = coarse_ref[pl.ds(c, 1), pl.ds(p * part, part)].astype(F32)
                prev = jnp.where(tag_b == c + 1.0, row, prev)
            resid[pl.ds(b * rows_b, rows_b), pl.ds(p * part, part)] = (
                flat[p * rows_b : (p + 1) * rows_b] - prev
            ).astype(BF16)
        prod_box[pl.ds(b * rows_b, rows_b), :] = lax.dot_general(
            resid[pl.ds(b * rows_b, rows_b), :],
            fines[...],
            (((1,), (1,)), ((), ())),
            preferred_element_type=F32,
        )

    prod = prod_box[...]
    logits = (prod - 0.5 * fsq) * scale
    cluster_of = (iota((1, group_fines), 1) >> 6).astype(F32) + 1.0
    logits = jnp.where(cluster_of == tag, logits, -1e30)
    top = jnp.max(logits, axis=1, keepdims=True)
    expo = jnp.exp(logits - top)
    valid = jnp.where(tag > 0.0, 1.0, 0.0)
    probs = expo / jnp.sum(expo, axis=1, keepdims=True) * valid

    tot_box[z] = jnp.sum(probs, axis=0, keepdims=True)
    for d in far_first(n_z):
        to = lax.rem(z + d, n_z)
        send(tot_box.at[z], tot_box.at[z], st_send.at[0], st_recv.at[0], own=to)

    weights = jnp.transpose(probs).astype(BF16)

    def chunk_stats(to):
        at = pl.multiple_of(to * cols, 128)
        return jnp.dot(weights, resid[:, pl.ds(at, cols)], preferred_element_type=F32)

    steps = (n_z // 2, n_z - 1 - n_z // 2)
    sub = group_fines // SUBS

    def target_of(way, t):
        off = steps[0] - t if way == 0 else n_z - steps[1] + t
        return lax.rem(z + off, n_z)

    def ring_send(way, t, s, src):
        to = lax.rem(z + (1 if way == 0 else n_z - 1), n_z)
        send(
            src,
            rs_buf.at[way, t, pl.ds(s * sub, sub)],
            rs_send.at[way, t, s],
            rs_recv.at[way, t, s],
            own=to,
        )

    def ring_first():
        for way in range(2):
            if steps[way] > 0:
                rs_src[way] = chunk_stats(target_of(way, 0)).astype(BF16)
                for s in range(SUBS):
                    ring_send(way, 0, s, rs_src.at[way, pl.ds(s * sub, sub)])

    def ring_step(t):
        for s in range(SUBS):
            for way in range(2):
                if t >= steps[way]:
                    continue
                held = rs_buf.at[way, t - 1, pl.ds(s * sub, sub)]
                drain(held, rs_recv.at[way, t - 1, s])
                add = stats[target_of(way, t), pl.ds(s * sub, sub), :]
                held[...] = (held[...].astype(F32) + add).astype(BF16)
                ring_send(way, t, s, held)

    ring_first()
    wide = part // cols
    for p in range(PARTS):
        quarter_stats = jnp.dot(
            weights, resid[:, pl.ds(p * part, part)], preferred_element_type=F32
        )
        for k in range(wide):
            stats[p * wide + k] = quarter_stats[:, k * cols : (k + 1) * cols]
    ring_step(1)
    ring_step(2)

    drain(tot_box.at[pl.ds(0, n_z - 1)], st_recv.at[0])
    totals = tot_box[0]
    for k in range(1, n_z):
        totals = totals + tot_box[k]
    tot_out[...] = totals
    tot_col = jnp.sum(jnp.where(eye_f, totals, 0.0), axis=1, keepdims=True)
    share = 1.0 / (4.0 + tot_col)
    mean_share = share * (1.0 / FINE_PER)

    def cluster_sum(value):
        return jnp.sum(value.reshape(CLU_DEV, FINE_PER, cols), axis=1)

    for p in range(PARTS):
        for k in range(wide):
            folded[pl.ds(k * CLU_DEV, CLU_DEV), :] = cluster_sum(stats[p * wide + k] * mean_share)
        cpart[p] = folded[...].astype(BF16)
    my_quarter = lax.rem(z, PARTS)
    cbox[z] = cpart[my_quarter]
    for d in far_first(n_z):
        to = lax.rem(z + d, n_z)
        send(cpart.at[lax.rem(to, PARTS)], cbox.at[z], st_send.at[1], st_recv.at[1], own=to)
    for k in range(wide):
        at = pl.ds(pl.multiple_of(my_quarter * part + k * cols, 128), cols)
        folded[pl.ds(k * CLU_DEV, CLU_DEV), :] = coarse_ref[:, at].astype(F32) + cluster_sum(
            4.0 * fines[:, at].astype(F32) * mean_share
        )
    ring_step(3)
    ring_step(4)

    drain(cbox.at[pl.ds(0, n_z - 1)], st_recv.at[1])
    piece = folded[...]
    for k in range(n_z):
        piece = piece + cbox[k].astype(F32)
    quarter_cols = pl.ds(pl.multiple_of(my_quarter * cols, 128), cols)
    mine = gath.at[core, x, y, :, quarter_cols]
    mine[...] = piece.astype(BF16)
    for k in [*far_first(n_y), 0]:
        dest = (x * n_y + lax.rem(y + n_y - k, n_y)) * 2 + core
        sem = st_send.at[2 if k else 5]
        if k:
            send(mine, mine, sem, y_recv.at[k], dp=dest)
        for d in quarter_to:
            send(mine, mine, sem, y_recv.at[k], dp=dest, own=lax.rem(z + d, n_z))

    ring_step(5)
    other = me + 1 - 2 * core
    for k in [0, *reversed(far_first(n_y))]:
        block = gath.at[core, x, lax.rem(y + k, n_y)]
        drain(block.at[:, pl.ds(0, (PARTS if k else PARTS - 1) * cols)], y_recv.at[k])
        for kx in far_first(n_x):
            dest = (lax.rem(x + kx, n_x) * n_y + y) * 2 + core
            send(block, block, st_send.at[3], x_recv.at[kx], dp=dest)
    ring_step(6)

    def pass_on(k):
        column = gath.at[core, lax.rem(x - k + n_x, n_x)]
        send(column, column, st_send.at[4], core_recv.at[k], dp=other)

    pass_on(0)
    for t in range(7, steps[0]):
        ring_step(t)
    near_x = [0, *reversed(far_first(n_x))]
    for k in near_x[1:]:
        drain(gath.at[core, lax.rem(x - k + n_x, n_x)], x_recv.at[k])
        pass_on(k)

    sums = stats[z]
    for way in range(2):
        if steps[way] > 0:
            for s in range(SUBS):
                last = steps[way] - 1
                drain(rs_buf.at[way, last, pl.ds(s * sub, sub)], rs_recv.at[way, last, s])
            sums = sums + rs_buf[way, steps[way] - 1].astype(F32)
    my_cols = pl.ds(pl.multiple_of(z * cols, 128), cols)
    fine_out[...] = (4.0 * fines[:, my_cols].astype(F32) + sums) * share


    blk = wide * CLU_DEV
    rows_x = 2 * n_y * CLU_DEV
    out_row = iota((rows_x * wide, rows_x * wide), 0)
    in_row = iota((rows_x * wide, rows_x * wide), 1)
    within = out_row & (rows_x - 1)
    from_block = ((within >> 2) & 1) * n_y + (within >> 3)
    at_cols = out_row >> (rows_x.bit_length() - 1)
    from_row = from_block * blk + at_cols * CLU_DEV + (within & 3)
    perm_x = (in_row == from_row).astype(F32).astype(BF16)
    for k in near_x:
        at = lax.rem(x - k + n_x, n_x)
        drain(gath.at[1 - core, at], core_recv.at[k])
        both = jnp.concatenate([gath[c, at, i] for c in range(2) for i in range(n_y)], axis=0)
        gathered = jnp.dot(perm_x, both, preferred_element_type=F32).astype(BF16)
        at_rows = pl.ds(pl.multiple_of(at * rows_x, rows_x), rows_x)
        for p in range(PARTS):
            for j in range(wide):
                coarse_out[at_rows, pl.ds(p * part + j * cols, cols)] = gathered[
                    j * rows_x : (j + 1) * rows_x, p * cols : (p + 1) * cols
                ]

    drain(ids_box.at[pl.ds(0, n_dp - 1)], ids_send)
    drain(outbox.at[pl.ds(0, (n_dp - 1) * BLK)], a2a_send)
    drain(tot_box.at[pl.ds(0, n_z - 1)], st_send.at[0])
    drain(cbox.at[pl.ds(0, n_z - 1)], st_send.at[1])
    drain(gath.at[0, 0, pl.ds(0, n_y - 1)], st_send.at[2])
    drain(gath.at[0, 0, 0, :, pl.ds(0, (PARTS - 1) * cols)], st_send.at[5])
    drain(gath.at[0, pl.ds(0, n_x - 1)], st_send.at[3])
    drain(gath.at[0], st_send.at[4])
    for way in range(2):
        for t in range(steps[way]):
            for s in range(SUBS):
                drain(rs_buf.at[way, t, pl.ds(s * sub, sub)], rs_send.at[way, t, s])


def store(fine, tot, coarse, fine_out, tot_out, coarse_out, sems):
    step = coarse.shape[0] // 4
    copies = [(fine, fine_out), (tot, tot_out)]
    for i in range(4):
        at = pl.ds(i * step, step)
        copies.append((coarse.at[at], coarse_out.at[at]))
    started = [pltpu.make_async_copy(a, b, sems.at[i]) for i, (a, b) in enumerate(copies)]
    for copy in started:
        copy.start()
    for copy in started:
        copy.wait()


def solution(mesh):
    n_dp, n_z = mesh.shape["dp"], mesh.shape["own"]
    n_x = N_X
    n_y = n_dp // (2 * n_x)

    def on_device(embeddings, coarse_ids, fine_cents, coarse_prev):
        rows, width = embeddings.shape
        group_fines = fine_cents.shape[0]
        cols = width // n_z
        part = width // PARTS
        blk = part // cols * CLU_DEV
        hbm = pl.BlockSpec(memory_space=pltpu.HBM)
        vmem = pl.BlockSpec(memory_space=pltpu.VMEM)
        dma = pltpu.SemaphoreType.DMA
        operands = (embeddings, coarse_ids.reshape(1, 1, rows), fine_cents, coarse_prev)
        operands = [pltpu.with_memory_space_constraint(a, pltpu.HBM) for a in operands]
        results = pl.pallas_call(
            functools.partial(kernel, n_x, n_y, n_z),
            out_shape=(
                pltpu.VMEM((group_fines, cols), F32),
                pltpu.VMEM((1, group_fines), F32),
                pltpu.VMEM((n_dp * CLU_DEV, width), BF16),
            ),
            in_specs=[hbm, hbm, hbm, hbm],
            out_specs=(vmem, vmem, vmem),
            scratch_shapes=[
                pltpu.VMEM((PARTS * rows, part), BF16),
                pltpu.VMEM((1, 1, rows), jnp.int32),
                pltpu.VMEM((group_fines, width), BF16),
                pltpu.VMEM((CLU_DEV, width), BF16),
                pltpu.VMEM((n_dp * BLK, part), BF16),
                pltpu.VMEM((n_dp * BLK, part), BF16),
                pltpu.VMEM((n_dp, 1, rows), jnp.int32),
                pltpu.VMEM((n_dp, rows), F32),
                pltpu.VMEM((n_dp * CAP, width), BF16),
                pltpu.VMEM((n_dp * CAP, group_fines), F32),
                pltpu.VMEM((n_z, group_fines, cols), F32),
                pltpu.VMEM((2, group_fines, cols), BF16),
                pltpu.VMEM((2, max(n_z // 2, 1), group_fines, cols), BF16),
                pltpu.VMEM((n_z, 1, group_fines), F32),
                pltpu.VMEM((PARTS, blk, cols), BF16),
                pltpu.VMEM((n_z, blk, cols), BF16),
                pltpu.VMEM((blk, cols), F32),
                pltpu.VMEM((2, n_x, n_y, blk, PARTS * cols), BF16),
                dma((PARTS + 3,)),
                dma(()),
                dma(()),
                dma(()),
                dma((n_x,)),
                dma((2, max(n_z // 2, 1), SUBS)),
                dma((2, max(n_z // 2, 1), SUBS)),
                dma((6,)),
                dma((2,)),
                dma((n_y,)),
                dma((n_x,)),
                dma((n_x,)),
            ],
            compiler_params=pltpu.CompilerParams(
                collective_id=0, has_side_effects=True, vmem_limit_bytes=40 * 2**20
            ),
        )(*operands)
        fine_next, totals, coarse_next = pl.pallas_call(
            store,
            out_shape=tuple(jax.ShapeDtypeStruct(a.shape, a.dtype) for a in results),
            in_specs=[vmem, vmem, vmem],
            out_specs=(hbm, hbm, hbm),
            scratch_shapes=[dma((6,))],
            compiler_params=pltpu.CompilerParams(vmem_limit_bytes=8 * 2**20),
        )(*results)
        return fine_next, totals.reshape(group_fines), coarse_next

    placed = (P(("dp", "own"), None), P(("dp", "own")), P("dp", None), P("dp", None))
    return jax.shard_map(
        on_device,
        mesh=mesh,
        in_specs=placed,
        out_specs=(P("dp", "own"), P("dp"), P()),
        check_vma=False,
    )
```

```python
import functools
import math

import jax
import jax.numpy as jnp
from jax import lax
from jax.experimental import pallas as pl
from jax.experimental.pallas import tpu as pltpu
from jax.sharding import PartitionSpec as P

MESH = pl.DeviceIdType.MESH
FINE_PER = 64
CLU_DEV = 4
CAP = 4
PARTS = 4
BLK = CAP * PARTS
N_X = 4
SUBS = 4
F32 = jnp.float32
BF16 = jnp.bfloat16


def drain(ref, sem):
    pltpu.make_async_copy(ref, ref, sem).wait()


def iota(shape, dim):
    return lax.broadcasted_iota(jnp.int32, shape, dim)


def kernel(
    n_x,
    n_y,
    n_z,
    emb_hbm,
    ids_hbm,
    fines_hbm,
    coarse_hbm,
    fine_out,
    tot_out,
    coarse_out,
    emb,
    ids_ref,
    fines,
    coarse_ref,
    outbox,
    inbox,
    ids_box,
    ids_f,
    resid,
    prod_box,
    stats,
    rs_src,
    rs_buf,
    tot_box,
    cpart,
    cbox,
    folded,
    gath,
    load_sem,
    ids_send,
    ids_recv,
    a2a_send,
    a2a_recv,
    rs_send,
    rs_recv,
    st_send,
    st_recv,
    y_recv,
    x_recv,
    core_recv,
):
    n_dp = 2 * n_x * n_y
    rows, width = emb_hbm.shape
    part = width // PARTS
    group_fines = fines.shape[0]
    cols = width // n_z
    scale = 4.0 / math.sqrt(width)

    me = lax.axis_index("dp")
    z = lax.axis_index("own")
    core = lax.rem(me, 2)
    chip = lax.div(me, 2)
    y = lax.rem(chip, n_y)
    x = lax.div(chip, n_y)

    def send(src, dst, send_sem, recv_sem, **to):
        copy = pltpu.make_async_remote_copy(
            src_ref=src,
            dst_ref=dst,
            send_sem=send_sem,
            recv_sem=recv_sem,
            device_id=to,
            device_id_type=MESH,
        )
        copy.start()

    def far_first(n):
        return sorted(range(1, n), key=lambda k: -min(k, n - k))

    barrier = pltpu.get_barrier_semaphore()

    loads = []
    for p in range(PARTS):
        loads.append(
            pltpu.make_async_copy(
                emb_hbm.at[:, pl.ds(p * part, part)],
                emb.at[pl.ds(p * rows, rows)],
                load_sem.at[p],
            )
        )
    loads.append(pltpu.make_async_copy(fines_hbm, fines, load_sem.at[PARTS]))
    loads.append(pltpu.make_async_copy(coarse_hbm, coarse_ref, load_sem.at[PARTS + 1]))
    load_ids = pltpu.make_async_copy(ids_hbm, ids_ref, load_sem.at[PARTS + 2])
    load_ids.start()
    for load in loads:
        load.start()

    @pl.loop(1, n_dp)
    def _(k):
        pl.semaphore_signal(
            barrier, inc=1, device_id={"dp": lax.rem(me + k, n_dp)}, device_id_type=MESH
        )

    @pl.loop(1, n_z)
    def _(k):
        pl.semaphore_signal(
            barrier, inc=1, device_id={"own": lax.rem(z + k, n_z)}, device_id_type=MESH
        )

    quarter_from = (1, n_z - 1, 2)
    quarter_to = (n_z - 1, 1, n_z - 2)

    @pl.loop(1, n_y)
    def _(k):
        dest = (x * n_y + lax.rem(y + k, n_y)) * 2 + core
        for d in quarter_from:
            pl.semaphore_signal(
                barrier,
                inc=1,
                device_id={"dp": dest, "own": lax.rem(z + d, n_z)},
                device_id_type=MESH,
            )

    load_ids.wait()
    ids = ids_ref[0]
    owner = ids >> 2
    owner_rows = jnp.broadcast_to(owner.astype(F32), (rows, rows))
    eye = iota((rows, rows), 0) == iota((rows, rows), 1)
    before = iota((rows, rows), 0) < iota((rows, rows), 1)
    owner_col = jnp.sum(jnp.where(eye, owner_rows, 0.0), axis=1, keepdims=True)
    same = jnp.where(before & (owner_col == owner_rows), 1.0, 0.0)
    rank = jnp.sum(same, axis=0, keepdims=True).astype(jnp.int32)
    y_bits = n_y.bit_length() - 1
    to_core = owner & 1
    to_y = (owner >> 1) & (n_y - 1)
    to_x = owner >> (1 + y_bits)
    dxi = (to_x - x + 2 * n_x - 1) & (n_x - 1)
    dy = (to_y - y + n_y) & (n_y - 1)
    half = n_y // 2
    dyi = jnp.where(dy >= half, 2 * (dy - half), 2 * (half - dy) - 1)
    place = ((to_core * n_x + dxi) * n_y + dyi) * BLK + rank
    target = jnp.concatenate([place + p * CAP for p in range(PARTS)], axis=1)

    ids_box[n_dp - 2] = ids
    for load in loads[:PARTS]:
        load.wait()
    chunk = n_y * BLK

    def build(jc):
        base = pl.multiple_of(jc * chunk, chunk)
        hot = (iota((chunk, PARTS * rows), 0) + base == target).astype(F32).astype(BF16)
        outbox[pl.ds(base, chunk), :] = jnp.dot(
            hot, emb[...], preferred_element_type=F32
        ).astype(BF16)

    build(0)
    pl.semaphore_wait(barrier, n_dp - 1 + n_z - 1 + 3 * (n_y - 1))

    @pl.loop(0, 2 * n_x)
    def _(jc):
        base = pl.multiple_of(jc * chunk, chunk)
        dest_core = lax.div(jc, n_x)
        at_x = lax.rem(jc, n_x)
        dest_x = lax.rem(x + at_x + 1, n_x)
        flip = lax.rem(dest_core + core, 2)
        for at_y in range(n_y):
            step = (at_y + 1) // 2
            delta = (n_y // 2 + (step if at_y % 2 == 0 else -step)) % n_y
            dest = (dest_x * n_y + lax.rem(y + delta, n_y)) * 2 + dest_core
            slot = (at_x * n_y + at_y) * 2 + flip
            src = outbox.at[pl.ds(pl.multiple_of(base + at_y * BLK, BLK), BLK)]
            dst = inbox.at[pl.ds(pl.multiple_of(slot * BLK, BLK), BLK)]

            def post():
                send(ids_ref.at[0], ids_box.at[slot], ids_send, ids_recv, dp=dest)
                send(src, dst, a2a_send, a2a_recv.at[at_x], dp=dest)

            if at_y < n_y - 1:
                post()
            else:
                mine = (at_x == n_x - 1) & (flip == 0)
                pl.when(jnp.logical_not(mine))(post)

                @pl.when(mine)
                def _():
                    pltpu.make_async_copy(src, dst, a2a_recv.at[at_x]).start()

        @pl.when(jc + 1 < 2 * n_x)
        def _():
            build(jc + 1)

    loads[PARTS].wait()
    loads[PARTS + 1].wait()
    fsq_col = jnp.sum(jnp.square(fines[...].astype(F32)), axis=1, keepdims=True)
    eye_f = iota((group_fines, group_fines), 0) == iota((group_fines, group_fines), 1)
    fsq = jnp.sum(jnp.where(eye_f, fsq_col, 0.0), axis=0, keepdims=True)

    drain(ids_box.at[pl.ds(0, n_dp - 1)], ids_recv)
    for i in range(n_dp):
        ids_f[pl.ds(i, 1), :] = ids_box[i].astype(F32)
    slots = n_dp * CAP
    spread = (iota((slots, n_dp), 0) >> 2) == iota((slots, n_dp), 1)
    seen = jnp.dot(
        spread.astype(F32).astype(BF16), ids_f[...].astype(BF16), preferred_element_type=F32
    )
    low = (me * CLU_DEV).astype(F32)
    ours = jnp.where((seen >= low) & (seen < low + CLU_DEV), 1.0, 0.0)
    order = jnp.dot(
        ours.astype(BF16), before.astype(F32).astype(BF16), preferred_element_type=F32
    )
    nth = (iota((slots, rows), 0) & (CAP - 1)).astype(F32)
    tag = jnp.sum(
        jnp.where(order == nth, ours * (seen - low + 1.0), 0.0), axis=1, keepdims=True
    )

    src_b = 2 * n_y
    rows_b = src_b * CAP
    out_row = iota((src_b * BLK, src_b * BLK), 0)
    in_row = iota((src_b * BLK, src_b * BLK), 1)
    quarter = out_row >> (rows_b.bit_length() - 1)
    within = out_row & (rows_b - 1)
    perm = (in_row == (within >> 2) * BLK + quarter * CAP + (within & 3)).astype(F32).astype(BF16)
    for b in range(n_x):
        arrived = inbox.at[pl.ds(b * src_b * BLK, src_b * BLK)]
        drain(arrived, a2a_recv.at[b])
        flat = jnp.dot(perm, arrived[...], preferred_element_type=F32)
        tag_b = tag[b * rows_b : (b + 1) * rows_b]
        for p in range(PARTS):
            prev = jnp.zeros((rows_b, part), F32)
            for c in range(CLU_DEV):
                row = coarse_ref[pl.ds(c, 1), pl.ds(p * part, part)].astype(F32)
                prev = jnp.where(tag_b == c + 1.0, row, prev)
            resid[pl.ds(b * rows_b, rows_b), pl.ds(p * part, part)] = (
                flat[p * rows_b : (p + 1) * rows_b] - prev
            ).astype(BF16)
        prod_box[pl.ds(b * rows_b, rows_b), :] = lax.dot_general(
            resid[pl.ds(b * rows_b, rows_b), :],
            fines[...],
            (((1,), (1,)), ((), ())),
            preferred_element_type=F32,
        )

    prod = prod_box[...]
    logits = (prod - 0.5 * fsq) * scale
    cluster_of = (iota((1, group_fines), 1) >> 6).astype(F32) + 1.0
    logits = jnp.where(cluster_of == tag, logits, -1e30)
    top = jnp.max(logits, axis=1, keepdims=True)
    expo = jnp.exp(logits - top)
    valid = jnp.where(tag > 0.0, 1.0, 0.0)
    probs = expo / jnp.sum(expo, axis=1, keepdims=True) * valid

    tot_box[z] = jnp.sum(probs, axis=0, keepdims=True)
    for d in far_first(n_z):
        to = lax.rem(z + d, n_z)
        send(tot_box.at[z], tot_box.at[z], st_send.at[0], st_recv.at[0], own=to)

    weights = jnp.transpose(probs).astype(BF16)

    def chunk_stats(to):
        at = pl.multiple_of(to * cols, 128)
        return jnp.dot(weights, resid[:, pl.ds(at, cols)], preferred_element_type=F32)

    steps = (n_z // 2, n_z - 1 - n_z // 2)
    sub = group_fines // SUBS

    def target_of(way, t):
        off = steps[0] - t if way == 0 else n_z - steps[1] + t
        return lax.rem(z + off, n_z)

    def ring_send(way, t, s, src):
        to = lax.rem(z + (1 if way == 0 else n_z - 1), n_z)
        send(
            src,
            rs_buf.at[way, t, pl.ds(s * sub, sub)],
            rs_send.at[way, t, s],
            rs_recv.at[way, t, s],
            own=to,
        )

    def ring_first():
        for way in range(2):
            if steps[way] > 0:
                rs_src[way] = chunk_stats(target_of(way, 0)).astype(BF16)
                for s in range(SUBS):
                    ring_send(way, 0, s, rs_src.at[way, pl.ds(s * sub, sub)])

    def ring_step(t):
        for s in range(SUBS):
            for way in range(2):
                if t >= steps[way]:
                    continue
                held = rs_buf.at[way, t - 1, pl.ds(s * sub, sub)]
                drain(held, rs_recv.at[way, t - 1, s])
                add = stats[target_of(way, t), pl.ds(s * sub, sub), :]
                held[...] = (held[...].astype(F32) + add).astype(BF16)
                ring_send(way, t, s, held)

    ring_first()
    wide = part // cols
    for p in range(PARTS):
        quarter_stats = jnp.dot(
            weights, resid[:, pl.ds(p * part, part)], preferred_element_type=F32
        )
        for k in range(wide):
            stats[p * wide + k] = quarter_stats[:, k * cols : (k + 1) * cols]
    ring_step(1)
    ring_step(2)

    drain(tot_box.at[pl.ds(0, n_z - 1)], st_recv.at[0])
    totals = tot_box[0]
    for k in range(1, n_z):
        totals = totals + tot_box[k]
    tot_out[...] = totals
    tot_col = jnp.sum(jnp.where(eye_f, totals, 0.0), axis=1, keepdims=True)
    share = 1.0 / (4.0 + tot_col)
    mean_share = share * (1.0 / FINE_PER)

    def cluster_sum(value):
        return jnp.sum(value.reshape(CLU_DEV, FINE_PER, cols), axis=1)

    my_quarter = lax.rem(z, PARTS)
    for i in (0, 3, 1, 2):
        q = lax.rem(z + i, PARTS)
        for k in range(wide):
            folded[pl.ds(k * CLU_DEV, CLU_DEV), :] = cluster_sum(stats[q * wide + k] * mean_share)
        cpart[q] = folded[...].astype(BF16)
        for d in far_first(n_z):
            if d % PARTS == i:
                to = lax.rem(z + d, n_z)
                send(cpart.at[q], cbox.at[z], st_send.at[1], st_recv.at[1], own=to)
    cbox[z] = cpart[my_quarter]
    for k in range(wide):
        at = pl.ds(pl.multiple_of(my_quarter * part + k * cols, 128), cols)
        folded[pl.ds(k * CLU_DEV, CLU_DEV), :] = coarse_ref[:, at].astype(F32) + cluster_sum(
            4.0 * fines[:, at].astype(F32) * mean_share
        )
    ring_step(3)
    ring_step(4)

    drain(cbox.at[pl.ds(0, n_z - 1)], st_recv.at[1])
    piece = folded[...]
    for k in range(n_z):
        piece = piece + cbox[k].astype(F32)
    quarter_cols = pl.ds(pl.multiple_of(my_quarter * cols, 128), cols)
    mine = gath.at[core, x, y, :, quarter_cols]
    mine[...] = piece.astype(BF16)
    for k in [*far_first(n_y), 0]:
        dest = (x * n_y + lax.rem(y + n_y - k, n_y)) * 2 + core
        sem = st_send.at[2 if k else 5]
        if k:
            send(mine, mine, sem, y_recv.at[k], dp=dest)
        for d in quarter_to:
            send(mine, mine, sem, y_recv.at[k], dp=dest, own=lax.rem(z + d, n_z))

    ring_step(5)
    other = me + 1 - 2 * core
    for k in [0, *reversed(far_first(n_y))]:
        block = gath.at[core, x, lax.rem(y + k, n_y)]
        drain(block.at[:, pl.ds(0, (PARTS if k else PARTS - 1) * cols)], y_recv.at[k])
        for kx in far_first(n_x):
            dest = (lax.rem(x + kx, n_x) * n_y + y) * 2 + core
            send(block, block, st_send.at[3], x_recv.at[kx], dp=dest)
    ring_step(6)

    def pass_on(k):
        column = gath.at[core, lax.rem(x - k + n_x, n_x)]
        send(column, column, st_send.at[4], core_recv.at[k], dp=other)

    pass_on(0)
    for t in range(7, steps[0]):
        ring_step(t)
    blk = wide * CLU_DEV
    rows_x = 2 * n_y * CLU_DEV
    out_row = iota((rows_x * wide, rows_x * wide), 0)
    in_row = iota((rows_x * wide, rows_x * wide), 1)
    within = out_row & (rows_x - 1)
    from_block = ((within >> 2) & 1) * n_y + (within >> 3)
    at_cols = out_row >> (rows_x.bit_length() - 1)
    from_row = from_block * blk + at_cols * CLU_DEV + (within & 3)
    perm_x = (in_row == from_row).astype(F32).astype(BF16)
    for k in [0, *reversed(far_first(n_x))]:
        at = lax.rem(x - k + n_x, n_x)
        if k:
            drain(gath.at[core, at], x_recv.at[k])
            pass_on(k)
        drain(gath.at[1 - core, at], core_recv.at[k])
        both = jnp.concatenate([gath[c, at, i] for c in range(2) for i in range(n_y)], axis=0)
        gathered = jnp.dot(perm_x, both, preferred_element_type=F32).astype(BF16)
        at_rows = pl.ds(pl.multiple_of(at * rows_x, rows_x), rows_x)
        for p in range(PARTS):
            for j in range(wide):
                coarse_out[at_rows, pl.ds(p * part + j * cols, cols)] = gathered[
                    j * rows_x : (j + 1) * rows_x, p * cols : (p + 1) * cols
                ]

    sums = stats[z]
    for way in range(2):
        if steps[way] > 0:
            for s in range(SUBS):
                last = steps[way] - 1
                drain(rs_buf.at[way, last, pl.ds(s * sub, sub)], rs_recv.at[way, last, s])
            sums = sums + rs_buf[way, steps[way] - 1].astype(F32)
    my_cols = pl.ds(pl.multiple_of(z * cols, 128), cols)
    fine_out[...] = (4.0 * fines[:, my_cols].astype(F32) + sums) * share

    drain(ids_box.at[pl.ds(0, n_dp - 1)], ids_send)
    drain(outbox.at[pl.ds(0, (n_dp - 1) * BLK)], a2a_send)
    drain(tot_box.at[pl.ds(0, n_z - 1)], st_send.at[0])
    drain(cbox.at[pl.ds(0, n_z - 1)], st_send.at[1])
    drain(gath.at[0, 0, pl.ds(0, n_y - 1)], st_send.at[2])
    drain(gath.at[0, 0, 0, :, pl.ds(0, (PARTS - 1) * cols)], st_send.at[5])
    drain(gath.at[0, pl.ds(0, n_x - 1)], st_send.at[3])
    drain(gath.at[0], st_send.at[4])
    for way in range(2):
        for t in range(steps[way]):
            for s in range(SUBS):
                drain(rs_buf.at[way, t, pl.ds(s * sub, sub)], rs_send.at[way, t, s])


def store(fine, tot, coarse, fine_out, tot_out, coarse_out, sems):
    step = coarse.shape[0] // 4
    copies = [(fine, fine_out), (tot, tot_out)]
    for i in range(4):
        at = pl.ds(i * step, step)
        copies.append((coarse.at[at], coarse_out.at[at]))
    started = [pltpu.make_async_copy(a, b, sems.at[i]) for i, (a, b) in enumerate(copies)]
    for copy in started:
        copy.start()
    for copy in started:
        copy.wait()


def solution(mesh):
    n_dp, n_z = mesh.shape["dp"], mesh.shape["own"]
    n_x = N_X
    n_y = n_dp // (2 * n_x)

    def on_device(embeddings, coarse_ids, fine_cents, coarse_prev):
        rows, width = embeddings.shape
        group_fines = fine_cents.shape[0]
        cols = width // n_z
        part = width // PARTS
        blk = part // cols * CLU_DEV
        hbm = pl.BlockSpec(memory_space=pltpu.HBM)
        vmem = pl.BlockSpec(memory_space=pltpu.VMEM)
        dma = pltpu.SemaphoreType.DMA
        operands = (embeddings, coarse_ids.reshape(1, 1, rows), fine_cents, coarse_prev)
        operands = [pltpu.with_memory_space_constraint(a, pltpu.HBM) for a in operands]
        results = pl.pallas_call(
            functools.partial(kernel, n_x, n_y, n_z),
            out_shape=(
                pltpu.VMEM((group_fines, cols), F32),
                pltpu.VMEM((1, group_fines), F32),
                pltpu.VMEM((n_dp * CLU_DEV, width), BF16),
            ),
            in_specs=[hbm, hbm, hbm, hbm],
            out_specs=(vmem, vmem, vmem),
            scratch_shapes=[
                pltpu.VMEM((PARTS * rows, part), BF16),
                pltpu.VMEM((1, 1, rows), jnp.int32),
                pltpu.VMEM((group_fines, width), BF16),
                pltpu.VMEM((CLU_DEV, width), BF16),
                pltpu.VMEM((n_dp * BLK, part), BF16),
                pltpu.VMEM((n_dp * BLK, part), BF16),
                pltpu.VMEM((n_dp, 1, rows), jnp.int32),
                pltpu.VMEM((n_dp, rows), F32),
                pltpu.VMEM((n_dp * CAP, width), BF16),
                pltpu.VMEM((n_dp * CAP, group_fines), F32),
                pltpu.VMEM((n_z, group_fines, cols), F32),
                pltpu.VMEM((2, group_fines, cols), BF16),
                pltpu.VMEM((2, max(n_z // 2, 1), group_fines, cols), BF16),
                pltpu.VMEM((n_z, 1, group_fines), F32),
                pltpu.VMEM((PARTS, blk, cols), BF16),
                pltpu.VMEM((n_z, blk, cols), BF16),
                pltpu.VMEM((blk, cols), F32),
                pltpu.VMEM((2, n_x, n_y, blk, PARTS * cols), BF16),
                dma((PARTS + 3,)),
                dma(()),
                dma(()),
                dma(()),
                dma((n_x,)),
                dma((2, max(n_z // 2, 1), SUBS)),
                dma((2, max(n_z // 2, 1), SUBS)),
                dma((6,)),
                dma((2,)),
                dma((n_y,)),
                dma((n_x,)),
                dma((n_x,)),
            ],
            compiler_params=pltpu.CompilerParams(
                collective_id=0, has_side_effects=True, vmem_limit_bytes=40 * 2**20
            ),
        )(*operands)
        fine_next, totals, coarse_next = pl.pallas_call(
            store,
            out_shape=tuple(jax.ShapeDtypeStruct(a.shape, a.dtype) for a in results),
            in_specs=[vmem, vmem, vmem],
            out_specs=(hbm, hbm, hbm),
            scratch_shapes=[dma((6,))],
            compiler_params=pltpu.CompilerParams(vmem_limit_bytes=8 * 2**20),
        )(*results)
        return fine_next, totals.reshape(group_fines), coarse_next

    placed = (P(("dp", "own"), None), P(("dp", "own")), P("dp", None), P("dp", None))
    return jax.shard_map(
        on_device,
        mesh=mesh,
        in_specs=placed,
        out_specs=(P("dp", "own"), P("dp"), P()),
        check_vma=False,
    )
```
